512 devices in a mesh: tm: 16 (over x_hi, z), seq: 32 (over x_lo, y, core).
Axes of the slice: x: 4 (x_hi: 2, x_lo: 2; x = x_hi * 2 + x_lo), y: 8, z: 8, core: 2. Of those that a mesh axis runs over, the one named last changes fastest.
Arguments:
- queries: bfloat16 [16, 2048, 4096], P('tm', 'seq'), may hold values from -80 to 80, as said below
- keys: bfloat16 [16, 2048, 4096], P('tm', 'seq'), may hold values from -5 to 5
- values: bfloat16 [16, 2048, 4096], P('tm', 'seq'), may hold values from -6 to 6
- text_kv: bfloat16 [2, 2, 512, 4096], P(None, None, None, 'seq'), may hold values from -6 to 6
- trajectory: bfloat16 [16, 2048, 4096], P('tm', 'seq'), may hold values from -6 to 6
- start_latent: bfloat16 [2048, 4096], P('seq'), may hold values from -6 to 6
- region_mask: int32 [64], replicated, may hold values from 0 to 1
- timesteps: int32 [16, 2], P('tm'), may hold values from 123 to 999
Outputs:
- updated: float32 [16, 2048, 4096], P('tm', 'seq')
The draws below stay inside these ranges and needn't reach their ends.
Inputs may be any that keep to these rules, and one draw needn't show every extreme that they name: `queries`: of order one and independent of the keys in the shown draw.
All inputs are finite; a program needn't handle non-finite values.
Results may differ from the reference program's by a relative error of at most 0.0009.
Values may be sent and summed in bfloat16 or wider, within the bound.
A program may use at most 64 MiB of HBM per device.

```python
import jax
import jax.numpy as jnp
from jax import lax

HD = 128
TEXT = 512
BLOCK = 32
HEADS = 32
F = 4096
TOKENS = 2048
STEPS = 16
NBLK = 64


def shared_keys(key):
    base = jax.random.normal(key, (STEPS, TOKENS, F), jnp.float32)
    return jnp.clip(base, -4.0, 4.0)


def draw_keys(key, part):
    base = shared_keys(key)
    return base.astype(jnp.bfloat16)


def draw_queries(key, part):
    key = jax.random.fold_in(key, 9)
    first_key = jax.random.fold_in(key, 0)
    fresh = jnp.clip(jax.random.normal(first_key, (STEPS, TOKENS, F), jnp.float32), -4.0, 4.0)
    return fresh.astype(jnp.bfloat16)


def draw_timesteps(key, part):
    key = jax.random.fold_in(key, 7)
    first_key, second_key = jax.random.split(key)
    current = jax.random.randint(first_key, (STEPS,), 250, 1000)
    current = jnp.where(jnp.arange(STEPS) == 0, 999, current)
    spacing = jax.random.randint(second_key, (STEPS,), 1, 128)
    return jnp.stack([current, current - spacing], axis=1).astype(jnp.int32)


def touch_ends(values, stream_key, least, high):
    spot = [jax.random.randint(jax.random.fold_in(stream_key, axis), (), 0, length) for axis, length in enumerate(values.shape)]
    longest = values.shape.index(max(values.shape))
    neighbour = spot[:longest] + [(spot[longest] + 1) % values.shape[longest]] + spot[longest + 1:]
    return values.at[tuple(spot)].set(least).at[tuple(neighbour)].set(high)


def block_levels(stream_key, extent, shards, low, largest):
    gain = 1.0
    for position, shards_of in shards:
        steps = jax.random.uniform(jax.random.fold_in(jax.random.fold_in(stream_key, 6), position), (shards_of,), jnp.float32, low / len(shards), largest / len(shards))
        gain = gain * jnp.repeat(jnp.exp(steps), extent[position] // shards_of).reshape((-1,) + (1,) * (len(extent) - 1 - position))
    return gain


def bell_draw(stream_key, shape, deviation, reach, pieces=(), held_as=jnp.bfloat16):
    array = deviation * jax.random.normal(stream_key, shape, jnp.float32)
    if pieces:
        array = array * block_levels(stream_key, shape, pieces, -0.22, 0.18)
    return jnp.clip(array, -reach, reach).astype(held_as)


def setup_inputs(seed: int = 0) -> dict:
    key_of = jax.random.split(jax.random.key(seed), 9)
    queries = draw_queries(jax.random.fold_in(key_of[8], 71), 0)
    keys = draw_keys(jax.random.fold_in(key_of[8], 71), 0)
    values = bell_draw(key_of[2], (STEPS, TOKENS, F), 1.0, 6.0, ((0, 16), (1, 32)))
    text_kv = bell_draw(key_of[3], (2, 2, TEXT, F), 1.0, 6.0, ((3, 32),))
    trajectory = bell_draw(key_of[4], (STEPS, TOKENS, F), 1.0, 6.0, ((0, 16), (1, 32)))
    start_latent = bell_draw(key_of[5], (TOKENS, F), 1.0, 6.0, ((0, 32),))
    region_mask = touch_ends(jax.random.randint(key_of[6], (NBLK,), 0, 2), jax.random.fold_in(key_of[6], 1), 0, 1).astype(jnp.int32)
    timesteps = draw_timesteps(jax.random.fold_in(key_of[8], 71), 0)
    return dict(queries=queries, keys=keys, values=values, text_kv=text_kv, trajectory=trajectory, start_latent=start_latent, region_mask=region_mask, timesteps=timesteps)


def attend(query_all, key_all, value_all, text_keys, text_values, heads_here, head_size):
    tokens = query_all.shape[0]
    row_count = min(512, tokens)
    block_count = tokens // row_count
    query_blocks = query_all.reshape(block_count, row_count, heads_here, head_size)
    key_heads = key_all.reshape(tokens, heads_here, head_size)
    value_heads = value_all.reshape(tokens, heads_here, head_size)
    text_key_heads = text_keys.reshape(2, -1, heads_here, head_size)
    text_value_heads = text_values.reshape(2, -1, heads_here, head_size)
    score_scale = head_size ** -0.5

    def one_block(query_block):
        video_score = jnp.einsum('rhd,khd->hrk', query_block, key_heads, preferred_element_type=jnp.float32) * score_scale
        text_score = jnp.einsum('rhd,bthd->bhrt', query_block, text_key_heads, preferred_element_type=jnp.float32) * score_scale
        row_top = jnp.maximum(jnp.max(video_score, axis=-1)[None], jnp.max(text_score, axis=-1))
        video_prob = jnp.exp(video_score[None] - row_top[..., None])
        text_prob = jnp.exp(text_score - row_top[..., None])
        summed = jnp.sum(video_prob, axis=-1) + jnp.sum(text_prob, axis=-1)
        video_weight = (video_prob / summed[..., None]).astype(jnp.bfloat16)
        text_weight = (text_prob / summed[..., None]).astype(jnp.bfloat16)
        result = jnp.einsum('bhrk,khd->brhd', video_weight, value_heads, preferred_element_type=jnp.float32)
        result = result + jnp.einsum('bhrt,bthd->brhd', text_weight, text_value_heads, preferred_element_type=jnp.float32)
        return result.astype(jnp.bfloat16)

    results = lax.map(one_block, query_blocks)
    return results.transpose(1, 0, 2, 3, 4).reshape(2, tokens, heads_here * head_size)


def guide_mix(cond_branch, uncond_branch, token_mask, noise_level):
    cond_part = cond_branch.astype(jnp.float32)
    uncond_part = uncond_branch.astype(jnp.float32)
    strength = 1.0 + 5.0 * noise_level
    blended = jnp.where(token_mask[:, None] > 0, uncond_part + strength * (cond_part - uncond_part), cond_part)
    return blended.astype(jnp.bfloat16)


def reference(queries, keys, values, text_kv, trajectory, start_latent, region_mask, timesteps):
    token_mask = jnp.repeat(region_mask, BLOCK)

    def one_step(inputs):
        query_step, key_step, value_step, latent_step, stamp = inputs
        branches = attend(query_step, key_step, value_step, text_kv[:, 0], text_kv[:, 1], HEADS, HD)
        noise_level = stamp[0].astype(jnp.float32) / 1000.0
        step_length = (stamp[1] - stamp[0]).astype(jnp.float32) / 1000.0
        guided = guide_mix(branches[0], branches[1], token_mask, noise_level)
        return step_length * ((latent_step.astype(jnp.float32) - guided.astype(jnp.float32)) / noise_level)

    drifts = lax.map(one_step, (queries, keys, values, trajectory, timesteps))
    return start_latent.astype(jnp.float32)[None] + jnp.cumsum(drifts, axis=0)
```

```python
import jax
import jax.numpy as jnp
from jax import lax
from jax.experimental import pallas as pl
from jax.experimental.pallas import tpu as pltpu
from jax.sharding import PartitionSpec as P

HD = 128
BLOCK = 32
TOK = 64
HALF = 32
NT = 32
NZ = 8
ROUNDS = 8
LAG1 = 1
LAG2 = 2
MESH = pl.DeviceIdType.MESH
F32 = jnp.float32
BF16 = jnp.bfloat16


def y_offset(r):
    half = (r + 1) // 2
    return jnp.where(r % 2 == 1, half, (8 - half) % 8)


def take_all(ref, sem):
    pltpu.make_async_copy(ref, ref, sem).wait()


def kernel(
    mask_ref, ts_ref, q_ref, k_ref, v_ref, text_ref, traj_ref, start_ref, out_ref,
    kbuf, vbuf, qbuf, text, gbuf, rbuf, pbuf, tjbuf, stbuf, totbuf, base, obuf, coef,
    k_sem, v_sem, q_sem, r_sem, p_sem, tj_sem, st_sem, tot_sem, o_sem, c_sem, text_sem,
    ks_sem, vs_sem, qs_sem, rs_sem, ps_sem, tjs_sem, tots_sem, os_sem, cs_sem,
):
    tm, seq = lax.axis_index("tm"), lax.axis_index("seq")
    xh, z = tm // NZ, tm % NZ
    x, y, c = seq // 16, (seq // 2) % 8, seq % 2
    mine = x * 2 + c

    def seq_peer(n):
        yy = (y + y_offset(n // 4)) % 8
        return ((x + (n // 2) % 2) % 2) * 16 + yy * 2 + (c + n % 2) % 2

    def columns(head):
        return pl.ds(pl.multiple_of(head * HD, HD), HD)

    def rows(index, size):
        return pl.ds(pl.multiple_of(index * size, size), size)

    barrier = pltpu.get_barrier_semaphore()

    def greet_seq(n, carry):
        pl.semaphore_signal(barrier, inc=1, device_id=(tm, seq_peer(n)), device_id_type=MESH)
        return carry

    def greet_z(n, carry):
        pl.semaphore_signal(
            barrier, inc=1, device_id=(xh * NZ + (z + n) % NZ, seq), device_id_type=MESH
        )
        return carry

    lax.fori_loop(1, NT, greet_seq, 0)
    lax.fori_loop(1, NZ, greet_z, 0)
    pl.semaphore_signal(barrier, inc=1, device_id=((1 - xh) * NZ + z, seq), device_id_type=MESH)

    role_a, role_h = z // 2, z % 2
    pltpu.make_async_copy(text_ref, text, text_sem).start()
    pltpu.make_async_copy(k_ref.at[:, columns(seq)], kbuf.at[rows(seq, TOK)], k_sem).start()
    pltpu.make_async_copy(v_ref.at[:, columns(seq)], vbuf.at[rows(seq, TOK)], v_sem).start()
    pltpu.make_async_copy(q_ref.at[:, columns(seq)], qbuf.at[0, mine], q_sem.at[0]).start()

    def head_of(a, r):
        return (a // 2) * 16 + ((y + y_offset(r)) % 8) * 2 + a % 2

    def local_tiles(r, carry):
        window = (rows(role_h, HALF), columns(head_of(role_a, r)))
        pltpu.make_async_copy(start_ref.at[window], stbuf.at[r], st_sem).start()
        pltpu.make_async_copy(traj_ref.at[window], tjbuf.at[r, z], tj_sem).start()
        return carry

    lax.fori_loop(0, ROUNDS, local_tiles, 0)

    now = jnp.full((8, HD), ts_ref[0, 0], jnp.int32).astype(F32)
    length = jnp.full((8, HD), ts_ref[0, 1] - ts_ref[0, 0], jnp.int32).astype(F32) / 1000.0
    noise = now / 1000.0
    strength = (1.0 + 5.0 * noise)[:1]
    coef[z] = length / noise

    pl.semaphore_wait(barrier, NT - 1 + NZ - 1 + 1)

    def send_k(n, carry):
        peer = seq_peer(n)
        pltpu.make_async_remote_copy(
            k_ref.at[:, columns(peer)], kbuf.at[rows(seq, TOK)], ks_sem, k_sem,
            device_id=(tm, peer), device_id_type=MESH,
        ).start()
        return carry

    def send_v(n, carry):
        peer = seq_peer(n)
        pltpu.make_async_remote_copy(
            v_ref.at[:, columns(peer)], vbuf.at[rows(seq, TOK)], vs_sem, v_sem,
            device_id=(tm, peer), device_id_type=MESH,
        ).start()
        return carry

    def send_q(n, carry):
        peer = seq_peer(n)
        pltpu.make_async_remote_copy(
            q_ref.at[:, columns(peer)], qbuf.at[n // 4, mine], qs_sem, q_sem.at[n // 4],
            device_id=(tm, peer), device_id_type=MESH,
        ).start()
        return carry

    def send_coef(n, carry):
        pltpu.make_async_remote_copy(
            coef.at[z], coef.at[z], cs_sem, c_sem,
            device_id=(xh * NZ + (z + n) % NZ, seq), device_id_type=MESH,
        ).start()
        return carry

    def send_traj(n, carry):
        other = (z + 1 + n // ROUNDS) % NZ
        r = n % ROUNDS
        window = (rows(other % 2, HALF), columns(head_of(other // 2, r)))
        pltpu.make_async_remote_copy(
            traj_ref.at[window], tjbuf.at[r, z], tjs_sem, tj_sem,
            device_id=(xh * NZ + other, seq), device_id_type=MESH,
        ).start()
        return carry

    lax.fori_loop(1, NT, send_k, 0)
    lax.fori_loop(1, NT, send_v, 0)
    lax.fori_loop(1, NZ, send_coef, 0)
    lax.fori_loop(1, NT, send_q, 0)
    lax.fori_loop(0, (NZ - 1) * ROUNDS, send_traj, 0)

    take_all(text_ref, text_sem)
    take_all(kbuf, k_sem)
    take_all(vbuf, v_sem)

    scale = HD ** (-0.5)
    nt = (((1,), (1,)), ((), ()))

    def attention(r):
        take_all(qbuf.at[r], q_sem.at[r])
        q = qbuf[r].reshape(4 * TOK, HD)
        sv = lax.dot_general(q, kbuf[...], nt, preferred_element_type=F32) * scale
        mv = jnp.max(sv, axis=-1, keepdims=True)
        pv = jnp.exp(sv - mv)
        lv = jnp.sum(pv, axis=-1, keepdims=True)
        branch = []
        for b in range(2):
            st = lax.dot_general(q, text[b, 0], nt, preferred_element_type=F32) * scale
            top = jnp.maximum(mv, jnp.max(st, axis=-1, keepdims=True))
            pt = jnp.exp(st - top)
            shift = jnp.exp(mv - top)
            inverse = 1.0 / (lv * shift + jnp.sum(pt, axis=-1, keepdims=True))
            wv = (pv * (shift * inverse)).astype(BF16)
            wt = (pt * inverse).astype(BF16)
            o = jnp.dot(wv, vbuf[...], preferred_element_type=F32)
            o = o + jnp.dot(wt, text[b, 1], preferred_element_type=F32)
            branch.append(o.astype(BF16).astype(F32))
        cond, uncond = branch
        mixed = uncond + strength * (cond - uncond)
        ys = (y + 8 - y_offset(r)) % 8
        for j in range(4):
            token_block = ((j // 2) * 16 + ys * 2 + j % 2) * 2
            for h in range(2):
                part = slice((2 * j + h) * BLOCK, (2 * j + h + 1) * BLOCK)
                guided_here = jnp.full((BLOCK, HD), mask_ref[token_block + h], jnp.int32) > 0
                gbuf[r, j, h * BLOCK : (h + 1) * BLOCK] = jnp.where(
                    guided_here, mixed[part], cond[part]
                ).astype(BF16)

        def send_back(j, carry):
            peer = (j // 2) * 16 + ys * 2 + j % 2

            @pl.when(peer == seq)
            def _():
                pltpu.make_async_copy(gbuf.at[r, j], rbuf.at[r, mine], r_sem.at[r]).start()

            @pl.when(peer != seq)
            def _():
                pltpu.make_async_remote_copy(
                    gbuf.at[r, j], rbuf.at[r, mine], rs_sem, r_sem.at[r],
                    device_id=(tm, peer), device_id_type=MESH,
                ).start()

            return carry

        lax.fori_loop(0, 4, send_back, 0)

    def to_steps(r):
        take_all(rbuf.at[r], r_sem.at[r])
        pltpu.make_async_copy(
            rbuf.at[r, role_a, rows(role_h, HALF)], pbuf.at[r, z], p_sem.at[r]
        ).start()

        def send(n, carry):
            other = (z + n) % NZ
            pltpu.make_async_remote_copy(
                rbuf.at[r, other // 2, rows(other % 2, HALF)], pbuf.at[r, z], ps_sem, p_sem.at[r],
                device_id=(xh * NZ + other, seq), device_id_type=MESH,
            ).start()
            return carry

        lax.fori_loop(1, NZ, send, 0)

    def running_sum(r):
        take_all(pbuf.at[r], p_sem.at[r])

        @pl.when(xh == 0)
        def _():
            base[...] = stbuf[r].astype(F32)

        @pl.when(xh == 1)
        def _():
            take_all(totbuf.at[r], tot_sem.at[r])
            base[...] = totbuf[r]

        total = base[...]
        for k in range(NZ):
            drift = coef[k, 0:1] * (tjbuf[r, k].astype(F32) - pbuf[r, k].astype(F32))
            total = total + drift
            obuf[r, k] = total

        @pl.when(xh == 0)
        def _():
            pltpu.make_async_remote_copy(
                obuf.at[r, NZ - 1], totbuf.at[r], tots_sem, tot_sem.at[r],
                device_id=(NZ + z, seq), device_id_type=MESH,
            ).start()

        window = (rows(role_h, HALF), columns(head_of(role_a, r)))
        pltpu.make_async_copy(obuf.at[r, z], out_ref.at[window], o_sem).start()

        def send(n, carry):
            other = (z + n) % NZ
            pltpu.make_async_remote_copy(
                obuf.at[r, other], out_ref.at[window], os_sem, o_sem,
                device_id=(xh * NZ + other, seq), device_id_type=MESH,
            ).start()
            return carry

        lax.fori_loop(1, NZ, send, 0)

    def turn(t, carry):
        @pl.when(t < ROUNDS)
        def _():
            attention(t)

        @pl.when((t >= LAG1) & (t < ROUNDS + LAG1))
        def _():
            to_steps(t - LAG1)

        @pl.when(t == LAG2)
        def _():
            take_all(stbuf, st_sem)
            take_all(tjbuf, tj_sem)
            take_all(coef.at[0 : NZ - 1], c_sem)

        @pl.when(t >= LAG2)
        def _():
            running_sum(t - LAG2)

        return carry

    lax.fori_loop(0, ROUNDS + LAG2, turn, 0)

    take_all(kbuf.at[0 : (NT - 1) * TOK], ks_sem)
    take_all(vbuf.at[0 : (NT - 1) * TOK], vs_sem)
    take_all(kbuf.at[0 : (NT - 1) * TOK], qs_sem)
    take_all(kbuf.at[0 : (NT - 1) * TOK], rs_sem)
    take_all(tjbuf.at[:, 0 : NZ - 1], tjs_sem)
    take_all(pbuf.at[:, 0 : NZ - 1], ps_sem)
    take_all(obuf.at[:, 0 : NZ - 1], os_sem)
    take_all(coef.at[0 : NZ - 1], cs_sem)

    @pl.when(xh == 0)
    def _():
        take_all(totbuf, tots_sem)

    take_all(out_ref, o_sem)


def per_device(queries, keys, values, text_kv, trajectory, start_latent, region_mask, timesteps):
    any_space = pl.BlockSpec(memory_space=pl.ANY)
    smem = pl.BlockSpec(memory_space=pltpu.SMEM)
    dma, dma8 = pltpu.SemaphoreType.DMA, pltpu.SemaphoreType.DMA((ROUNDS,))
    out = pl.pallas_call(
        kernel,
        out_shape=jax.ShapeDtypeStruct(queries.shape[1:], F32),
        in_specs=[smem, smem] + [any_space] * 6,
        out_specs=any_space,
        scratch_shapes=[
            pltpu.VMEM((NT * TOK, HD), BF16),
            pltpu.VMEM((NT * TOK, HD), BF16),
            pltpu.VMEM((ROUNDS, 4, TOK, HD), BF16),
            pltpu.VMEM(text_kv.shape, BF16),
            pltpu.VMEM((ROUNDS, 4, TOK, HD), BF16),
            pltpu.VMEM((ROUNDS, 4, TOK, HD), BF16),
            pltpu.VMEM((ROUNDS, NZ, HALF, HD), BF16),
            pltpu.VMEM((ROUNDS, NZ, HALF, HD), BF16),
            pltpu.VMEM((ROUNDS, HALF, HD), BF16),
            pltpu.VMEM((ROUNDS, HALF, HD), F32),
            pltpu.VMEM((HALF, HD), F32),
            pltpu.VMEM((ROUNDS, NZ, HALF, HD), F32),
            pltpu.VMEM((NZ, 8, HD), F32),
            dma, dma, dma8, dma8, dma8, dma, dma, dma8, dma, dma, dma,
            dma, dma, dma, dma, dma, dma, dma, dma, dma,
        ],
        compiler_params=pltpu.CompilerParams(
            collective_id=0, has_side_effects=True, vmem_limit_bytes=48 << 20
        ),
    )(
        region_mask, timesteps, queries[0], keys[0], values[0], text_kv, trajectory[0], start_latent
    )
    return out[None]


def solution(mesh):
    return jax.shard_map(
        per_device,
        mesh=mesh,
        in_specs=(
            P("tm", "seq", None),
            P("tm", "seq", None),
            P("tm", "seq", None),
            P(None, None, None, "seq"),
            P("tm", "seq", None),
            P("seq", None),
            P(),
            P("tm", None),
        ),
        out_specs=P("tm", "seq", None),
        check_vma=False,
    )
```

```python
import math

import jax
import jax.numpy as jnp
from jax import lax
from jax.experimental import pallas as pl
from jax.experimental.pallas import tpu as pltpu
from jax.sharding import PartitionSpec as P

HD = 128
BLOCK = 32
TOK = 64
HALF = 32
NT = 32
NZ = 8
ROUNDS = 8
LAGS = (0, 2, 4, 6, 8)
BEHIND = 2
MESH = pl.DeviceIdType.MESH
F32 = jnp.float32
BF16 = jnp.bfloat16


def y_offset(r):
    half = (r + 1) // 2
    return jnp.where(r % 2 == 1, half, (8 - half) % 8)


def take_all(ref, sem):
    pltpu.make_async_copy(ref, ref, sem).wait()


def kernel(
    mask_ref, ts_ref, q_ref, k_ref, v_ref, text_ref, traj_ref, start_ref, out_ref,
    mask, ts, kbuf, vbuf, qbuf, text, own, gbuf, rbuf, pbuf, tjbuf, stbuf, totbuf, base, sums, last,
    fin, obuf, coef,
    small_sem, k_sem, v_sem, q_sem, r_sem, p_sem, tj_sem, st_sem, tot_sem, f_sem, l_sem, o_sem,
    c_sem, text_sem, own_sem,
    ks_sem, vs_sem, qs_sem, rs_sem, ps_sem, tjs_sem, tots_sem, fs_sem, ls_sem, cs_sem,
):
    tm, seq = lax.axis_index("tm"), lax.axis_index("seq")
    xh, z = tm // NZ, tm % NZ
    x, y, c = seq // 16, (seq // 2) % 8, seq % 2
    mine = x * 2 + c

    def seq_peer(n):
        yy = (y + y_offset(n // 4)) % 8
        return ((x + (n // 2) % 2) % 2) * 16 + yy * 2 + (c + n % 2) % 2

    def columns(head):
        return pl.ds(pl.multiple_of(head * HD, HD), HD)

    def rows(index, size):
        return pl.ds(pl.multiple_of(index * size, size), size)

    barrier = pltpu.get_barrier_semaphore()

    def greet_seq(n, carry):
        pl.semaphore_signal(barrier, inc=1, device_id=(tm, seq_peer(n)), device_id_type=MESH)
        return carry

    def greet_z(n, carry):
        pl.semaphore_signal(
            barrier, inc=1, device_id=(xh * NZ + (z + n) % NZ, seq), device_id_type=MESH
        )
        return carry

    lax.fori_loop(1, NT, greet_seq, 0)
    lax.fori_loop(1, NZ, greet_z, 0)
    pl.semaphore_signal(barrier, inc=1, device_id=((1 - xh) * NZ + z, seq), device_id_type=MESH)

    role_a, role_h = z // 2, z % 2
    partner = z + 1 - 2 * role_h
    pltpu.make_async_copy(mask_ref, mask, small_sem.at[0]).start()
    pltpu.make_async_copy(ts_ref, ts, small_sem.at[1]).start()
    pltpu.make_async_copy(traj_ref, own, own_sem).start()
    pltpu.make_async_copy(text_ref, text, text_sem).start()
    pltpu.make_async_copy(k_ref.at[:, columns(seq)], kbuf.at[rows(seq, TOK)], k_sem).start()
    pltpu.make_async_copy(v_ref.at[:, columns(seq)], vbuf.at[rows(seq, TOK)], v_sem).start()
    pltpu.make_async_copy(q_ref.at[:, columns(seq)], qbuf.at[0, mine], q_sem.at[0]).start()

    def head_of(a, r):
        return (a // 2) * 16 + ((y + y_offset(r)) % 8) * 2 + a % 2

    def local_tiles(r, carry):
        window = (rows(role_h, HALF), columns(head_of(role_a, r)))
        pltpu.make_async_copy(start_ref.at[window], stbuf.at[r], st_sem).start()
        pltpu.make_async_copy(traj_ref.at[window], tjbuf.at[r, z], tj_sem).start()
        return carry

    lax.fori_loop(0, ROUNDS, local_tiles, 0)

    pltpu.make_async_copy(mask_ref, mask, small_sem.at[0]).wait()
    pltpu.make_async_copy(ts_ref, ts, small_sem.at[1]).wait()

    now = jnp.full((8, HD), ts[0, 0], jnp.int32).astype(F32)
    length = jnp.full((8, HD), ts[0, 1] - ts[0, 0], jnp.int32).astype(F32) / 1000.0
    noise = now / 1000.0
    strength = (1.0 + 5.0 * noise)[:1]
    coef[z] = length / noise

    pl.semaphore_wait(barrier, NT - 1 + NZ - 1 + 1)

    def send_k(n, carry):
        peer = seq_peer(NT - n)
        pltpu.make_async_remote_copy(
            k_ref.at[:, columns(peer)], kbuf.at[rows(seq, TOK)], ks_sem, k_sem,
            device_id=(tm, peer), device_id_type=MESH,
        ).start()
        return carry

    def send_v(n, carry):
        peer = seq_peer(NT - n)
        pltpu.make_async_remote_copy(
            v_ref.at[:, columns(peer)], vbuf.at[rows(seq, TOK)], vs_sem, v_sem,
            device_id=(tm, peer), device_id_type=MESH,
        ).start()
        return carry

    def send_q(n, carry):
        peer = seq_peer(n)
        pltpu.make_async_remote_copy(
            q_ref.at[:, columns(peer)], qbuf.at[n // 4, mine], qs_sem, q_sem.at[n // 4],
            device_id=(tm, peer), device_id_type=MESH,
        ).start()
        return carry

    def send_coef(n, carry):
        pltpu.make_async_remote_copy(
            coef.at[z], coef.at[z], cs_sem, c_sem,
            device_id=(xh * NZ + (z + n) % NZ, seq), device_id_type=MESH,
        ).start()
        return carry

    def send_traj(n, carry):
        other = (z + 1 + n // ROUNDS) % NZ
        r = n % ROUNDS
        window = (rows(other % 2, HALF), columns(head_of(other // 2, r)))
        pltpu.make_async_remote_copy(
            traj_ref.at[window], tjbuf.at[r, z], tjs_sem, tj_sem,
            device_id=(xh * NZ + other, seq), device_id_type=MESH,
        ).start()
        return carry

    lax.fori_loop(1, NT, send_k, 0)
    lax.fori_loop(1, NT, send_v, 0)
    lax.fori_loop(1, NZ, send_coef, 0)
    lax.fori_loop(1, NT, send_q, 0)
    lax.fori_loop(0, (NZ - 1) * ROUNDS, send_traj, 0)

    take_all(text_ref, text_sem)
    take_all(kbuf, k_sem)
    take_all(vbuf, v_sem)

    scale = HD ** (-0.5) * math.log2(math.e)
    nt = (((1,), (1,)), ((), ()))

    def attention(r):
        take_all(qbuf.at[r], q_sem.at[r])
        q = qbuf[r].reshape(4 * TOK, HD)
        halves = [q[: 2 * TOK], q[2 * TOK :]]
        scores = [
            [lax.dot_general(h, k, nt, preferred_element_type=F32) for k in (kbuf[...], text[0, 0], text[1, 0])]
            for h in halves
        ]
        branch = [[], []]
        for sv, *st in scores:
            mv = jnp.max(sv, axis=-1, keepdims=True)
            pv = jnp.exp2((sv - mv) * scale)
            lv = jnp.sum(pv, axis=-1, keepdims=True)
            for b in range(2):
                top = jnp.maximum(mv, jnp.max(st[b], axis=-1, keepdims=True))
                pt = jnp.exp2((st[b] - top) * scale)
                shift = jnp.exp2((mv - top) * scale)
                inverse = 1.0 / (lv * shift + jnp.sum(pt, axis=-1, keepdims=True))
                wv = (pv * (shift * inverse)).astype(BF16)
                wt = (pt * inverse).astype(BF16)
                o = jnp.dot(wv, vbuf[...], preferred_element_type=F32)
                o = o + jnp.dot(wt, text[b, 1], preferred_element_type=F32)
                branch[b].append(o.astype(BF16).astype(F32))
        branch = [jnp.concatenate(halves, axis=0) for halves in branch]
        cond, uncond = branch
        mixed = uncond + strength * (cond - uncond)
        ys = (y + 8 - y_offset(r)) % 8
        for j in range(4):
            token_block = ((j // 2) * 16 + ys * 2 + j % 2) * 2
            for h in range(2):
                part = slice((2 * j + h) * BLOCK, (2 * j + h + 1) * BLOCK)
                guided_here = jnp.full((BLOCK, HD), mask[token_block + h], jnp.int32) > 0
                gbuf[r, j, h * BLOCK : (h + 1) * BLOCK] = jnp.where(
                    guided_here, mixed[part], cond[part]
                ).astype(BF16)

        def send_back(j, carry):
            peer = (j // 2) * 16 + ys * 2 + j % 2

            @pl.when(peer == seq)
            def _():
                pltpu.make_async_copy(gbuf.at[r, j], rbuf.at[r, mine], r_sem.at[r]).start()

            @pl.when(peer != seq)
            def _():
                pltpu.make_async_remote_copy(
                    gbuf.at[r, j], rbuf.at[r, mine], rs_sem, r_sem.at[r],
                    device_id=(tm, peer), device_id_type=MESH,
                ).start()

            return carry

        lax.fori_loop(0, 4, send_back, 0)

    def to_steps(r):
        take_all(rbuf.at[r], r_sem.at[r])
        pltpu.make_async_copy(
            rbuf.at[r, role_a, rows(role_h, HALF)], pbuf.at[r, z], p_sem.at[r]
        ).start()

        def send(n, carry):
            other = (z + n) % NZ
            pltpu.make_async_remote_copy(
                rbuf.at[r, other // 2, rows(other % 2, HALF)], pbuf.at[r, z], ps_sem, p_sem.at[r],
                device_id=(xh * NZ + other, seq), device_id_type=MESH,
            ).start()
            return carry

        lax.fori_loop(1, NZ, send, 0)

    def running_sum(r):
        take_all(pbuf.at[r], p_sem.at[r])

        @pl.when(xh == 0)
        def _():
            base[...] = stbuf[r].astype(F32)

        @pl.when(xh == 1)
        def _():
            take_all(totbuf.at[r], tot_sem.at[r])
            base[...] = totbuf[r]

        total = base[...]
        for k in range(NZ):
            drift = coef[k, 0:1] * (tjbuf[r, k].astype(F32) - pbuf[r, k].astype(F32))
            total = total + drift
            if k % 2 == 0:
                sums[r, k // 2] = total
        last[r] = total

        @pl.when(xh == 0)
        def _():
            pltpu.make_async_remote_copy(
                last.at[r], totbuf.at[r], tots_sem, tot_sem.at[r],
                device_id=(NZ + z, seq), device_id_type=MESH,
            ).start()

        def send(other):
            pltpu.make_async_remote_copy(
                sums.at[r, other // 2], fin.at[r, z], fs_sem, f_sem.at[r],
                device_id=(xh * NZ + other, seq), device_id_type=MESH,
            ).start()

        @pl.when(role_h == 0)
        def _():
            send((z + 5) % NZ)
            send((z + 2) % NZ)
            send((z + 7) % NZ)
            send(z + 1)

        @pl.when(role_h == 1)
        def _():
            send((z + 3) % NZ)
            send((z + 6) % NZ)
            send((z + 1) % NZ)
            send(z - 1)

        fin[r, z] = sums[r, role_a]

    def relay(r):
        take_all(fin.at[r, 0:4], f_sem.at[r])

        def send(n, carry):
            role = (z + NZ + (2 * role_h - 1) * n) % NZ
            pltpu.make_async_remote_copy(
                fin.at[r, role], fin.at[r, role], ls_sem, l_sem.at[r],
                device_id=(xh * NZ + partner, seq), device_id_type=MESH,
            ).start()
            return carry

        lax.fori_loop(1, 4, send, 0)

    def finish(r):
        take_all(fin.at[r, 0:3], l_sem.at[r])
        for a in range(4):
            head = head_of(a, r)
            state = fin[r, 2 * a : 2 * a + 2].reshape(TOK, HD)
            latent = own[:, columns(head)].astype(F32)
            drift = coef[z, 0:1] * (latent - rbuf[r, a].astype(F32))
            odd = jnp.full((TOK, HD), role_h, jnp.int32) > 0
            obuf[r, a] = jnp.where(odd, state + drift, state)
            pltpu.make_async_copy(obuf.at[r, a], out_ref.at[:, columns(head)], o_sem).start()

    stages = (attention, to_steps, running_sum, relay, finish)

    def turn(t, carry):
        @pl.when(t == 2)
        def _():
            take_all(stbuf, st_sem)
            take_all(tjbuf, tj_sem)
            take_all(coef.at[0 : NZ - 1], c_sem)
            take_all(own, own_sem)

        for lag, stage in zip(LAGS, stages):
            if lag >= LAGS[2]:
                lag = lag + xh * BEHIND

            @pl.when((t >= lag) & (t < ROUNDS + lag))
            def _(lag=lag, stage=stage):
                stage(t - lag)

        return carry

    lax.fori_loop(0, ROUNDS + LAGS[-1] + BEHIND, turn, 0)

    take_all(kbuf.at[0 : (NT - 1) * TOK], ks_sem)
    take_all(vbuf.at[0 : (NT - 1) * TOK], vs_sem)
    take_all(kbuf.at[0 : (NT - 1) * TOK], qs_sem)
    take_all(kbuf.at[0 : (NT - 1) * TOK], rs_sem)
    take_all(tjbuf.at[:, 0 : NZ - 1], tjs_sem)
    take_all(pbuf.at[:, 0 : NZ - 1], ps_sem)
    take_all(sums, fs_sem)
    take_all(fin.at[:, 0:3], ls_sem)
    take_all(coef.at[0 : NZ - 1], cs_sem)

    @pl.when(xh == 0)
    def _():
        take_all(totbuf, tots_sem)

    take_all(out_ref, o_sem)


def per_device(queries, keys, values, text_kv, trajectory, start_latent, region_mask, timesteps):
    any_space = pl.BlockSpec(memory_space=pl.ANY)
    dma, dma8 = pltpu.SemaphoreType.DMA, pltpu.SemaphoreType.DMA((ROUNDS,))
    out = pl.pallas_call(
        kernel,
        out_shape=jax.ShapeDtypeStruct(queries.shape[1:], F32),
        in_specs=[any_space] * 8,
        out_specs=any_space,
        scratch_shapes=[
            pltpu.SMEM(region_mask.shape, jnp.int32),
            pltpu.SMEM(timesteps.shape, jnp.int32),
            pltpu.VMEM((NT * TOK, HD), BF16),
            pltpu.VMEM((NT * TOK, HD), BF16),
            pltpu.VMEM((ROUNDS, 4, TOK, HD), BF16),
            pltpu.VMEM(text_kv.shape, BF16),
            pltpu.VMEM(trajectory.shape[1:], BF16),
            pltpu.VMEM((ROUNDS, 4, TOK, HD), BF16),
            pltpu.VMEM((ROUNDS, 4, TOK, HD), BF16),
            pltpu.VMEM((ROUNDS, NZ, HALF, HD), BF16),
            pltpu.VMEM((ROUNDS, NZ, HALF, HD), BF16),
            pltpu.VMEM((ROUNDS, HALF, HD), BF16),
            pltpu.VMEM((ROUNDS, HALF, HD), F32),
            pltpu.VMEM((HALF, HD), F32),
            pltpu.VMEM((ROUNDS, NZ // 2, HALF, HD), F32),
            pltpu.VMEM((ROUNDS, HALF, HD), F32),
            pltpu.VMEM((ROUNDS, NZ, HALF, HD), F32),
            pltpu.VMEM((ROUNDS, 4, TOK, HD), F32),
            pltpu.VMEM((NZ, 8, HD), F32),
            pltpu.SemaphoreType.DMA((2,)),
            dma, dma, dma8, dma8, dma8, dma, dma, dma8, dma8, dma8, dma,
            dma, dma, dma,
            dma, dma, dma, dma, dma, dma, dma, dma, dma, dma,
        ],
        compiler_params=pltpu.CompilerParams(
            collective_id=0, has_side_effects=True, vmem_limit_bytes=62 << 20
        ),
    )(
        region_mask, timesteps, queries[0], keys[0], values[0], text_kv, trajectory[0], start_latent
    )
    return out[None]


def solution(mesh):
    return jax.shard_map(
        per_device,
        mesh=mesh,
        in_specs=(
            P("tm", "seq", None),
            P("tm", "seq", None),
            P("tm", "seq", None),
            P(None, None, None, "seq"),
            P("tm", "seq", None),
            P("seq", None),
            P(),
            P("tm", None),
        ),
        out_specs=P("tm", "seq", None),
        check_vma=False,
    )
```

```python
import math

import jax
import jax.numpy as jnp
from jax import lax
from jax.experimental import pallas as pl
from jax.experimental.pallas import tpu as pltpu
from jax.sharding import PartitionSpec as P

HD = 128
BLOCK = 32
TOK = 64
HALF = 32
NT = 32
NZ = 8
ROUNDS = 8
LAGS = (0, 3, 5, 7, 9)
DIRECT = 6
BEHIND = 1
MESH = pl.DeviceIdType.MESH
F32 = jnp.float32
BF16 = jnp.bfloat16


def y_offset(r):
    half = (r + 1) // 2
    return jnp.where(r % 2 == 1, half, (8 - half) % 8)


def take_all(ref, sem):
    pltpu.make_async_copy(ref, ref, sem).wait()


def kernel(
    mask_ref, ts_ref, q_ref, k_ref, v_ref, text_ref, traj_ref, start_ref, out_ref,
    mask, ts, kbuf, vbuf, qbuf, text, own, gbuf, rbuf, pbuf, tjbuf, stbuf, totbuf, base, sums, last,
    fin, obuf, coef,
    small_sem, k_sem, v_sem, q_sem, r_sem, p_sem, tj_sem, st_sem, tot_sem, f_sem, l_sem, o_sem,
    c_sem, text_sem, own_sem,
    ks_sem, vs_sem, qs_sem, rs_sem, ps_sem, tjs_sem, tots_sem, fs_sem, ds_sem, ls_sem, cs_sem,
):
    tm, seq = lax.axis_index("tm"), lax.axis_index("seq")
    xh, z = tm // NZ, tm % NZ
    x, y, c = seq // 16, (seq // 2) % 8, seq % 2
    mine = x * 2 + c

    def seq_peer(n):
        yy = (y + y_offset(n // 4)) % 8
        return ((x + (n // 2) % 2) % 2) * 16 + yy * 2 + (c + n % 2) % 2

    def columns(head):
        return pl.ds(pl.multiple_of(head * HD, HD), HD)

    def rows(index, size):
        return pl.ds(pl.multiple_of(index * size, size), size)

    barrier = pltpu.get_barrier_semaphore()

    def greet_seq(n, carry):
        pl.semaphore_signal(barrier, inc=1, device_id=(tm, seq_peer(n)), device_id_type=MESH)
        return carry

    def greet_z(n, carry):
        pl.semaphore_signal(
            barrier, inc=1, device_id=(xh * NZ + (z + n) % NZ, seq), device_id_type=MESH
        )
        return carry

    lax.fori_loop(1, NT, greet_seq, 0)
    lax.fori_loop(1, NZ, greet_z, 0)
    pl.semaphore_signal(barrier, inc=1, device_id=((1 - xh) * NZ + z, seq), device_id_type=MESH)

    role_a, role_h = z // 2, z % 2
    partner = z + 1 - 2 * role_h
    pltpu.make_async_copy(mask_ref, mask, small_sem.at[0]).start()
    pltpu.make_async_copy(ts_ref, ts, small_sem.at[1]).start()
    pltpu.make_async_copy(traj_ref, own, own_sem).start()
    pltpu.make_async_copy(text_ref, text, text_sem).start()
    pltpu.make_async_copy(k_ref.at[:, columns(seq)], kbuf.at[rows(seq, TOK)], k_sem).start()
    pltpu.make_async_copy(v_ref.at[:, columns(seq)], vbuf.at[rows(seq, TOK)], v_sem).start()
    pltpu.make_async_copy(q_ref.at[:, columns(seq)], qbuf.at[0, mine], q_sem.at[0]).start()

    def head_of(a, r):
        return (a // 2) * 16 + ((y + y_offset(r)) % 8) * 2 + a % 2

    def local_tiles(r, carry):
        window = (rows(role_h, HALF), columns(head_of(role_a, r)))
        pltpu.make_async_copy(start_ref.at[window], stbuf.at[r], st_sem).start()
        pltpu.make_async_copy(traj_ref.at[window], tjbuf.at[r, z], tj_sem).start()
        return carry

    lax.fori_loop(0, ROUNDS, local_tiles, 0)

    pltpu.make_async_copy(mask_ref, mask, small_sem.at[0]).wait()
    pltpu.make_async_copy(ts_ref, ts, small_sem.at[1]).wait()

    now = jnp.full((8, HD), ts[0, 0], jnp.int32).astype(F32)
    length = jnp.full((8, HD), ts[0, 1] - ts[0, 0], jnp.int32).astype(F32) / 1000.0
    noise = now / 1000.0
    strength = (1.0 + 5.0 * noise)[:1]
    coef[z] = length / noise

    pl.semaphore_wait(barrier, NT - 1 + NZ - 1 + 1)

    def send_k(n, carry):
        peer = seq_peer(NT - n)
        pltpu.make_async_remote_copy(
            k_ref.at[:, columns(peer)], kbuf.at[rows(seq, TOK)], ks_sem, k_sem,
            device_id=(tm, peer), device_id_type=MESH,
        ).start()
        return carry

    def send_v(n, carry):
        peer = seq_peer(NT - n)
        pltpu.make_async_remote_copy(
            v_ref.at[:, columns(peer)], vbuf.at[rows(seq, TOK)], vs_sem, v_sem,
            device_id=(tm, peer), device_id_type=MESH,
        ).start()
        return carry

    def send_q(n, carry):
        peer = seq_peer(n)
        pltpu.make_async_remote_copy(
            q_ref.at[:, columns(peer)], qbuf.at[n // 4, mine], qs_sem, q_sem.at[n // 4],
            device_id=(tm, peer), device_id_type=MESH,
        ).start()
        return carry

    def send_coef(n, carry):
        pltpu.make_async_remote_copy(
            coef.at[z], coef.at[z], cs_sem, c_sem,
            device_id=(xh * NZ + (z + n) % NZ, seq), device_id_type=MESH,
        ).start()
        return carry

    def send_traj(n, carry):
        other = (z + 1 + n // ROUNDS) % NZ
        r = n % ROUNDS
        window = (rows(other % 2, HALF), columns(head_of(other // 2, r)))
        pltpu.make_async_remote_copy(
            traj_ref.at[window], tjbuf.at[r, z], tjs_sem, tj_sem,
            device_id=(xh * NZ + other, seq), device_id_type=MESH,
        ).start()
        return carry

    lax.fori_loop(1, NT, send_k, 0)
    lax.fori_loop(1, NT, send_v, 0)
    lax.fori_loop(1, NZ, send_coef, 0)
    lax.fori_loop(1, NT, send_q, 0)
    lax.fori_loop(0, (NZ - 1) * ROUNDS, send_traj, 0)

    take_all(text_ref, text_sem)
    take_all(kbuf, k_sem)
    take_all(vbuf, v_sem)

    scale = HD ** (-0.5) * math.log2(math.e)
    nt = (((1,), (1,)), ((), ()))

    def attention(r):
        take_all(qbuf.at[r], q_sem.at[r])
        q = qbuf[r].reshape(4 * TOK, HD)
        halves = [q[: 2 * TOK], q[2 * TOK :]]
        scores = [
            [lax.dot_general(h, k, nt, preferred_element_type=F32) for k in (kbuf[...], text[0, 0], text[1, 0])]
            for h in halves
        ]
        branch = [[], []]
        for sv, *st in scores:
            mv = jnp.max(sv, axis=-1, keepdims=True)
            pv = jnp.exp2((sv - mv) * scale)
            lv = jnp.sum(pv, axis=-1, keepdims=True)
            for b in range(2):
                top = jnp.maximum(mv, jnp.max(st[b], axis=-1, keepdims=True))
                pt = jnp.exp2((st[b] - top) * scale)
                shift = jnp.exp2((mv - top) * scale)
                inverse = 1.0 / (lv * shift + jnp.sum(pt, axis=-1, keepdims=True))
                wv = (pv * (shift * inverse)).astype(BF16)
                wt = (pt * inverse).astype(BF16)
                o = jnp.dot(wv, vbuf[...], preferred_element_type=F32)
                o = o + jnp.dot(wt, text[b, 1], preferred_element_type=F32)
                branch[b].append(o.astype(BF16).astype(F32))
        branch = [jnp.concatenate(halves, axis=0) for halves in branch]
        cond, uncond = branch
        mixed = uncond + strength * (cond - uncond)
        ys = (y + 8 - y_offset(r)) % 8
        for j in range(4):
            token_block = ((j // 2) * 16 + ys * 2 + j % 2) * 2
            for h in range(2):
                part = slice((2 * j + h) * BLOCK, (2 * j + h + 1) * BLOCK)
                guided_here = jnp.full((BLOCK, HD), mask[token_block + h], jnp.int32) > 0
                gbuf[r, j, h * BLOCK : (h + 1) * BLOCK] = jnp.where(
                    guided_here, mixed[part], cond[part]
                ).astype(BF16)

        def send_back(j, carry):
            peer = (j // 2) * 16 + ys * 2 + j % 2

            @pl.when(peer == seq)
            def _():
                pltpu.make_async_copy(gbuf.at[r, j], rbuf.at[r, mine], r_sem.at[r]).start()

            @pl.when(peer != seq)
            def _():
                pltpu.make_async_remote_copy(
                    gbuf.at[r, j], rbuf.at[r, mine], rs_sem, r_sem.at[r],
                    device_id=(tm, peer), device_id_type=MESH,
                ).start()

            return carry

        lax.fori_loop(0, 4, send_back, 0)

    def to_steps(r):
        take_all(rbuf.at[r], r_sem.at[r])
        pltpu.make_async_copy(
            rbuf.at[r, role_a, rows(role_h, HALF)], pbuf.at[r, z], p_sem.at[r]
        ).start()

        def send(n, carry):
            other = (z + n) % NZ
            pltpu.make_async_remote_copy(
                rbuf.at[r, other // 2, rows(other % 2, HALF)], pbuf.at[r, z], ps_sem, p_sem.at[r],
                device_id=(xh * NZ + other, seq), device_id_type=MESH,
            ).start()
            return carry

        lax.fori_loop(1, NZ, send, 0)

    def running_sum(r):
        take_all(pbuf.at[r], p_sem.at[r])

        @pl.when(xh == 0)
        def _():
            base[...] = stbuf[r].astype(F32)

        @pl.when(xh == 1)
        def _():
            take_all(totbuf.at[r], tot_sem.at[r])
            base[...] = totbuf[r]

        total = base[...]
        for k in range(NZ):
            drift = coef[k, 0:1] * (tjbuf[r, k].astype(F32) - pbuf[r, k].astype(F32))
            total = total + drift
            if k % 2 == 0:
                sums[r, k // 2] = total
        last[r] = total

        @pl.when(xh == 0)
        def _():
            pltpu.make_async_remote_copy(
                last.at[r], totbuf.at[r], tots_sem, tot_sem.at[r],
                device_id=(NZ + z, seq), device_id_type=MESH,
            ).start()

        def send(other, sent=fs_sem):
            pltpu.make_async_remote_copy(
                sums.at[r, other // 2], fin.at[r, z], sent, f_sem.at[r],
                device_id=(xh * NZ + other, seq), device_id_type=MESH,
            ).start()

        @pl.when((r < DIRECT) & (role_h == 0))
        def _():
            send((z + 5) % NZ)
            send((z + 2) % NZ)
            send((z + 7) % NZ)
            send(z + 1)

        @pl.when((r < DIRECT) & (role_h == 1))
        def _():
            send((z + 3) % NZ)
            send((z + 6) % NZ)
            send((z + 1) % NZ)
            send(z - 1)

        @pl.when(r >= DIRECT)
        def _():
            def send_to(n, carry):
                send((z + n) % NZ, ds_sem)
                return carry

            lax.fori_loop(1, NZ, send_to, 0)

        fin[r, z] = sums[r, role_a]

    def relay(r):
        @pl.when(r < DIRECT)
        def _():
            take_all(fin.at[r, 0:4], f_sem.at[r])

            def send(n, carry):
                role = (z + NZ + (2 * role_h - 1) * n) % NZ
                pltpu.make_async_remote_copy(
                    fin.at[r, role], fin.at[r, role], ls_sem, l_sem.at[r],
                    device_id=(xh * NZ + partner, seq), device_id_type=MESH,
                ).start()
                return carry

            lax.fori_loop(1, 4, send, 0)

    def finish(r):
        @pl.when(r < DIRECT)
        def _():
            take_all(fin.at[r, 0:3], l_sem.at[r])

        @pl.when(r >= DIRECT)
        def _():
            take_all(fin.at[r, 0 : NZ - 1], f_sem.at[r])

        for a in range(4):
            head = head_of(a, r)
            state = fin[r, 2 * a : 2 * a + 2].reshape(TOK, HD)
            latent = own[:, columns(head)].astype(F32)
            drift = coef[z, 0:1] * (latent - rbuf[r, a].astype(F32))
            odd = jnp.full((TOK, HD), role_h, jnp.int32) > 0
            obuf[r, a] = jnp.where(odd, state + drift, state)
            pltpu.make_async_copy(obuf.at[r, a], out_ref.at[:, columns(head)], o_sem).start()

    stages = (attention, to_steps, running_sum, relay, finish)

    def turn(t, carry):
        @pl.when(t == 2)
        def _():
            take_all(stbuf, st_sem)
            take_all(tjbuf, tj_sem)
            take_all(coef.at[0 : NZ - 1], c_sem)
            take_all(own, own_sem)

        for lag, stage in zip(LAGS, stages):
            if lag >= LAGS[2]:
                lag = lag + xh * BEHIND

            @pl.when((t >= lag) & (t < ROUNDS + lag))
            def _(lag=lag, stage=stage):
                stage(t - lag)

        return carry

    lax.fori_loop(0, ROUNDS + LAGS[-1] + BEHIND, turn, 0)

    take_all(kbuf.at[0 : (NT - 1) * TOK], ks_sem)
    take_all(vbuf.at[0 : (NT - 1) * TOK], vs_sem)
    take_all(kbuf.at[0 : (NT - 1) * TOK], qs_sem)
    take_all(kbuf.at[0 : (NT - 1) * TOK], rs_sem)
    take_all(tjbuf.at[:, 0 : NZ - 1], tjs_sem)
    take_all(pbuf.at[:, 0 : NZ - 1], ps_sem)
    take_all(sums.at[0:DIRECT], fs_sem)
    take_all(fin.at[0 : ROUNDS - DIRECT, 0 : NZ - 1], ds_sem)
    take_all(fin.at[0:DIRECT, 0:3], ls_sem)
    take_all(coef.at[0 : NZ - 1], cs_sem)

    @pl.when(xh == 0)
    def _():
        take_all(totbuf, tots_sem)

    take_all(out_ref, o_sem)


def per_device(queries, keys, values, text_kv, trajectory, start_latent, region_mask, timesteps):
    any_space = pl.BlockSpec(memory_space=pl.ANY)
    dma, dma8 = pltpu.SemaphoreType.DMA, pltpu.SemaphoreType.DMA((ROUNDS,))
    out = pl.pallas_call(
        kernel,
        out_shape=jax.ShapeDtypeStruct(queries.shape[1:], F32),
        in_specs=[any_space] * 8,
        out_specs=any_space,
        scratch_shapes=[
            pltpu.SMEM(region_mask.shape, jnp.int32),
            pltpu.SMEM(timesteps.shape, jnp.int32),
            pltpu.VMEM((NT * TOK, HD), BF16),
            pltpu.VMEM((NT * TOK, HD), BF16),
            pltpu.VMEM((ROUNDS, 4, TOK, HD), BF16),
            pltpu.VMEM(text_kv.shape, BF16),
            pltpu.VMEM(trajectory.shape[1:], BF16),
            pltpu.VMEM((ROUNDS, 4, TOK, HD), BF16),
            pltpu.VMEM((ROUNDS, 4, TOK, HD), BF16),
            pltpu.VMEM((ROUNDS, NZ, HALF, HD), BF16),
            pltpu.VMEM((ROUNDS, NZ, HALF, HD), BF16),
            pltpu.VMEM((ROUNDS, HALF, HD), BF16),
            pltpu.VMEM((ROUNDS, HALF, HD), F32),
            pltpu.VMEM((HALF, HD), F32),
            pltpu.VMEM((ROUNDS, NZ // 2, HALF, HD), F32),
            pltpu.VMEM((ROUNDS, HALF, HD), F32),
            pltpu.VMEM((ROUNDS, NZ, HALF, HD), F32),
            pltpu.VMEM((ROUNDS, 4, TOK, HD), F32),
            pltpu.VMEM((NZ, 8, HD), F32),
            pltpu.SemaphoreType.DMA((2,)),
            dma, dma, dma8, dma8, dma8, dma, dma, dma8, dma8, dma8, dma,
            dma, dma, dma,
            dma, dma, dma, dma, dma, dma, dma, dma, dma, dma, dma,
        ],
        compiler_params=pltpu.CompilerParams(
            collective_id=0, has_side_effects=True, vmem_limit_bytes=62 << 20
        ),
    )(
        region_mask, timesteps, queries[0], keys[0], values[0], text_kv, trajectory[0], start_latent
    )
    return out[None]


def solution(mesh):
    return jax.shard_map(
        per_device,
        mesh=mesh,
        in_specs=(
            P("tm", "seq", None),
            P("tm", "seq", None),
            P("tm", "seq", None),
            P(None, None, None, "seq"),
            P("tm", "seq", None),
            P("seq", None),
            P(),
            P("tm", None),
        ),
        out_specs=P("tm", "seq", None),
        check_vma=False,
    )
```
